32 devices in a mesh: groups: 2 (over y), row: 4 (over z), col: 2 (over x), sub: 2 (over core).
Axes of the slice: x: 2, y: 2, z: 4, core: 2. Of those that a mesh axis runs over, the one named last changes fastest.
Arguments:
- object_field: float32 [2, 4096, 512], P(None, ('groups', 'row', 'sub'), 'col'), parts along dimension 1, may hold values from -5 to 5
- probe_field: float32 [4, 256, 256], P('groups'), parts along dimension 0, may hold values from -5 to 5
- patterns: float32 [96, 256, 256], P(('groups', 'row', 'col', 'sub')), parts along dimension 0, may hold values from 0.1 to 3
- offset_rows: int32 [96], P(('groups', 'row', 'col', 'sub')), parts along dimension 0, may hold values from 0 to 1792, as said below
- offset_cols: int32 [96], P(('groups', 'row', 'col', 'sub')), parts along dimension 0, may hold values from 0 to 256, as said below
- counts: int32 [32], P(('groups', 'row', 'col', 'sub')), parts along dimension 0, may hold values from 1 to 3, as said below
- fresnel: float32 [1], replicated, may hold values from 0.05 to 0.5
- object_step: float32 [1], replicated, may hold values from 1 to 4
- probe_step: float32 [1], replicated, may hold values from 2 to 8
Outputs:
- object_out: float32 [2, 4096, 512], P(None, ('groups', 'row', 'sub'), 'col'), parts along dimension 1
- probe_out: float32 [4, 256, 256], P('groups'), parts along dimension 0
The draws below stay inside these ranges and needn't reach their ends.
There are 2 independent parts, one for each index of `groups`. The reference program is written for one: setup_inputs(seed, part) draws one part's arguments, and reference() takes and returns one part's arrays. A program takes and returns all parts, laid end to end along the dimension named above; an argument that names none is the same for every part. Nothing has to cross between parts.
Inputs may be any that keep to these rules, and one draw needn't show every extreme that they name: `offset_rows`: position p belongs to owner p // 3, owners counted in the mesh order row, col, sub; its first row lies in that owner's object tile rows (tiles of 256 rows ordered by row, then sub) and its patch stays inside the object. `offset_cols`: its first column lies in the owner's tile columns (tiles of 256 columns ordered by col) and its patch stays inside the object. `counts`: an owner's live positions are its first slots.
All inputs are finite; a program needn't handle non-finite values.
Results may differ from the reference program's by a relative error of at most 0.0003.
Values sent between devices are 32-bit elements; how exact they have to be, the bound alone decides.
A program may use at most 64 MiB of HBM per device.

```python
import math
import jax
import jax.numpy as jnp
from jax import lax

PATCH = 256
TILE_R = 256
TILE_C = 256
SLOTS = 3
ITERS = 2
OWNERS = 16
POSITIONS = 48
NX = 2048
NY = 512
N_ROW = 4
N_COL = 2
N_SUB = 2


def draw_offset_rows(key, part):
    key = jax.random.fold_in(key, 11)
    position_count = SLOTS * OWNERS
    position_ids = jnp.arange(position_count, dtype=jnp.int32)
    owner_id = position_ids // SLOTS
    tile_row = owner_id // (N_COL * N_SUB) * N_SUB + owner_id % N_SUB
    at_end = tile_row == N_ROW * N_SUB - 1
    span_len = jnp.where(at_end, TILE_R - PATCH + 1, TILE_R)
    drawn_rows = jax.random.randint(key, (position_count,), 0, 1 << 20) % span_len
    chosen = at_end & (owner_id // N_SUB % N_COL == 0) & (position_ids % SLOTS == 0)
    within = jnp.where(chosen, TILE_R - PATCH, drawn_rows)
    return (tile_row * TILE_R + within).astype(jnp.int32)


def draw_offset_cols(key, part):
    key = jax.random.fold_in(key, 12)
    position_count = SLOTS * OWNERS
    position_ids = jnp.arange(position_count, dtype=jnp.int32)
    owner_id = position_ids // SLOTS
    tile_col = owner_id // N_SUB % N_COL
    at_end = tile_col == N_COL - 1
    span_len = jnp.where(at_end, TILE_C - PATCH + 1, TILE_C)
    drawn_cols = jax.random.randint(key, (position_count,), 0, 1 << 20) % span_len
    chosen = at_end & (owner_id // (N_COL * N_SUB) == 0) & (owner_id % N_SUB == 0) & (position_ids % SLOTS == 0)
    within = jnp.where(chosen, TILE_C - PATCH, drawn_cols)
    return (tile_col * TILE_C + within).astype(jnp.int32)


def draw_counts(key, part):
    key = jax.random.fold_in(key, 13)
    sub_keys = jax.random.split(key, 3)
    light_count = 1 + jax.random.randint(sub_keys[0], (OWNERS,), 0, max(SLOTS - 1, 1))
    is_heavy = jax.random.randint(sub_keys[1], (OWNERS,), 0, 8) == 0
    drawn_counts = jnp.where(is_heavy, SLOTS, light_count)
    picked = jax.random.randint(sub_keys[2], (), 0, OWNERS)
    owner_ids = jnp.arange(OWNERS, dtype=jnp.int32)
    drawn_counts = jnp.where(owner_ids == picked, SLOTS, drawn_counts)
    drawn_counts = jnp.where(owner_ids == (picked + 1) % OWNERS, 1, drawn_counts)
    return drawn_counts.astype(jnp.int32)


def levels(stream_key, extent, cuts, least, high):
    def one(dim, shards_of):
        draws = jax.random.uniform(jax.random.fold_in(jax.random.fold_in(stream_key, 6), dim), (shards_of,), jnp.float32, least / len(cuts), high / len(cuts))
        return jnp.repeat(jnp.exp(draws), extent[dim] // shards_of).reshape((-1,) + (1,) * (len(extent) - dim - 1))

    factor_of = one(*cuts[0])
    for cut in cuts[1:]:
        factor_of = factor_of * one(*cut)
    return factor_of


def normal_values(key, shape, width, limit, cuts=(), kind=jnp.bfloat16):
    loudness = levels(key, shape, cuts, -0.22, 0.18) if cuts else 1.0
    result = jax.random.normal(key, shape, jnp.float32) * width * loudness
    return jnp.minimum(jnp.maximum(result, -limit), limit).astype(kind)


def setup_inputs(seed: int = 0, part: int = 0) -> dict:
    key_list = jax.random.split(jax.random.key(seed), 10)
    part_keys = jax.random.split(jax.random.fold_in(key_list[9], part), 10)
    return {
        "object_field": normal_values(part_keys[0], (2, NX, NY), 0.7, 5.0, ((1, 8), (2, 2)), jnp.float32),
        "probe_field": normal_values(part_keys[1], (2, PATCH, PATCH), 0.7, 5.0, (), jnp.float32),
        "patterns": jnp.clip(jnp.exp(math.log(3.0) - 3.4011974 * jax.random.uniform(part_keys[2], (POSITIONS, PATCH, PATCH), jnp.float32) ** levels(part_keys[2], (POSITIONS, PATCH, PATCH), ((0, 16),), -0.2, 0.2)), 0.1, 3.0),
        "offset_rows": draw_offset_rows(jax.random.fold_in(jax.random.fold_in(key_list[9], part), 71), part),
        "offset_cols": draw_offset_cols(jax.random.fold_in(jax.random.fold_in(key_list[9], part), 71), part),
        "counts": draw_counts(jax.random.fold_in(jax.random.fold_in(key_list[9], part), 71), part),
        "fresnel": jnp.clip(jnp.exp(jax.random.uniform(key_list[6], (1,), jnp.float32, math.log(0.05), math.log(0.5))), 0.05, 0.5),
        "object_step": jnp.clip(jnp.exp(jax.random.uniform(key_list[7], (1,), jnp.float32, math.log(1.0), math.log(4.0))), 1.0, 4.0),
        "probe_step": jnp.clip(jnp.exp(jax.random.uniform(key_list[8], (1,), jnp.float32, math.log(2.0), math.log(8.0))), 2.0, 8.0),
    }


HIGHEST = lax.Precision.HIGHEST


def propagator(fresnel, pixels):
    positions = jnp.arange(pixels, dtype=jnp.int32)
    product = (positions[:, None] * positions[None, :]) % pixels
    angles = (2.0 * math.pi / pixels) * product.astype(jnp.float32)
    cosine = jnp.cos(angles)
    sine_table = jnp.sin(angles)
    frequency = jnp.where(positions < pixels // 2, positions, positions - pixels).astype(jnp.float32)
    phases = (-math.pi / pixels) * fresnel[0] * frequency * frequency
    trans_r = jnp.cos(phases)
    trans_i = jnp.sin(phases)
    left_r = (cosine * trans_r[None, :] - sine_table * trans_i[None, :]) / pixels
    left_i = (cosine * trans_i[None, :] + sine_table * trans_r[None, :]) / pixels
    kern_r = jnp.dot(left_r, cosine, precision=HIGHEST) + jnp.dot(left_i, sine_table, precision=HIGHEST)
    kern_i = jnp.dot(left_i, cosine, precision=HIGHEST) - jnp.dot(left_r, sine_table, precision=HIGHEST)
    return kern_r, kern_i


def apply_left(matrix, field):
    return jnp.einsum("mn,snk->smk", matrix, field, precision=HIGHEST)


def apply_right(field, matrix):
    return jnp.einsum("smn,nk->smk", field, matrix, precision=HIGHEST)


def propagate(kern_r, kern_i, field_r, field_i):
    middle_r = apply_left(kern_r, field_r) - apply_left(kern_i, field_i)
    middle_i = apply_left(kern_r, field_i) + apply_left(kern_i, field_r)
    out_r = apply_right(middle_r, kern_r) - apply_right(middle_i, kern_i)
    out_i = apply_right(middle_r, kern_i) + apply_right(middle_i, kern_r)
    return out_r, out_i


def reference(object_field, probe_field, patterns, offset_rows, offset_cols, counts, fresnel, object_step, probe_step):
    kern_r, kern_i = propagator(fresnel, PATCH)
    active = (jnp.arange(SLOTS, dtype=jnp.int32)[None, :] < counts[:, None]).reshape(-1).astype(jnp.float32)
    for sweep_index in range(ITERS):
        probe_r = probe_field[0]
        probe_i = probe_field[1]
        current_object = object_field

        def visit(carry, item):
            grad_object, grad_probe, weight = carry
            row_at, col_at, pattern, alive = item
            corner = (jnp.int32(0), row_at.astype(jnp.int32), col_at.astype(jnp.int32))
            patch = lax.dynamic_slice(current_object, corner, (2, PATCH, PATCH))
            obj_r = patch[0][None]
            obj_i = patch[1][None]
            exit_r = probe_r * obj_r - probe_i * obj_i
            exit_i = probe_r * obj_i + probe_i * obj_r
            wave_r, wave_i = propagate(kern_r, kern_i, exit_r, exit_i)
            excess = (wave_r * wave_r + wave_i * wave_i - pattern[None]) * alive
            back_r, back_i = propagate(kern_r, -kern_i, excess * wave_r, excess * wave_i)
            back_r = back_r[0]
            back_i = back_i[0]
            term = jnp.stack([probe_r * back_r + probe_i * back_i, probe_r * back_i - probe_i * back_r])
            existing = lax.dynamic_slice(grad_object, corner, (2, PATCH, PATCH))
            grad_object = lax.dynamic_update_slice(grad_object, existing + term, corner)
            grad_probe = grad_probe + jnp.stack([obj_r[0] * back_r + obj_i[0] * back_i, obj_r[0] * back_i - obj_i[0] * back_r])
            weight = weight + alive * (obj_r[0] * obj_r[0] + obj_i[0] * obj_i[0])
            return (grad_object, grad_probe, weight), None

        start = (jnp.zeros(object_field.shape, jnp.float32), jnp.zeros(probe_field.shape, jnp.float32), jnp.zeros((PATCH, PATCH), jnp.float32))
        (grad_object, grad_probe, weight), unused = lax.scan(visit, start, (offset_rows, offset_cols, patterns, active))
        largest = jnp.max(probe_r * probe_r + probe_i * probe_i)
        object_field = object_field - (object_step[0] / (largest + 1e-6)) * grad_object
        probe_field = probe_field - probe_step[0] * grad_probe / (weight + 1.0)
    return object_field, probe_field
```

```python
import functools
import math

import jax
import jax.numpy as jnp
import numpy as np
from jax import lax
from jax.experimental import pallas as pl
from jax.experimental.pallas import tpu as pltpu
from jax.sharding import PartitionSpec as P

ITERS = 2
CHUNKS = 4
HIGHEST = lax.Precision.HIGHEST
MESH = pl.DeviceIdType.MESH


def split(value):
    high = value.astype(jnp.bfloat16)
    return high, (value - high.astype(jnp.float32)).astype(jnp.bfloat16)


def build_propagator(n, fresnel_ref, cosine_ref, sine_ref, left_ref, right_ref):
    freq = lax.broadcasted_iota(jnp.int32, (8, n), 1)
    freq = jnp.where(freq < n // 2, freq, freq - n).astype(jnp.float32)
    phases = -math.pi / n * fresnel_ref[0] * freq * freq
    trans_r = jnp.cos(phases)[0:1]
    trans_i = jnp.sin(phases)[0:1]
    cosine = cosine_ref[...]
    sine = sine_ref[...]
    half_r = (cosine * trans_r - sine * trans_i) * (1.0 / n)
    half_i = (cosine * trans_i + sine * trans_r) * (1.0 / n)

    def exact(a, b):
        return jnp.dot(a, b, precision=HIGHEST, preferred_element_type=jnp.float32)

    kern_r = exact(half_r, cosine) + exact(half_i, sine)
    kern_i = exact(half_i, cosine) - exact(half_r, sine)
    r_high, r_low = split(kern_r)
    i_high, i_low = split(kern_i)
    for part, (r_half, i_half) in enumerate(((r_high, i_high), (r_low, i_low), (r_high, i_high))):
        base = part * 2 * n
        left_ref[:n, base : base + n] = r_half
        left_ref[:n, base + n : base + 2 * n] = -i_half
        left_ref[n:, base : base + n] = i_half
        left_ref[n:, base + n : base + 2 * n] = r_half
        right_ref[base : base + n, :n] = r_half
        right_ref[base : base + n, n:] = i_half
        right_ref[base + n : base + 2 * n, :n] = -i_half
        right_ref[base + n : base + 2 * n, n:] = r_half


def gradients(
    sizes,
    rows_ref,
    cols_ref,
    counts_ref,
    region,
    probe,
    patterns_ref,
    left_ref,
    right_ref,
    grad,
    partial,
    padded,
    stacked,
    patch_ref,
):
    n_sub = sizes[2]
    slots, n = patterns_ref.shape[0], patterns_ref.shape[1]
    tile = lax.axis_index("row") * n_sub + lax.axis_index("sub")
    col = lax.axis_index("col")

    def propagate(x_r, x_i):
        for k, value in enumerate((x_r, x_i)):
            high, low = split(value)
            stacked[k * n : (k + 1) * n, :] = high
            stacked[(k + 2) * n : (k + 3) * n, :] = high
            stacked[(k + 4) * n : (k + 5) * n, :] = low
        mid = jnp.dot(left_ref[...], stacked[...], preferred_element_type=jnp.float32)
        a_high, a_low = split(mid[:n])
        b_high, b_low = split(mid[n:])
        wide = jnp.concatenate([a_high, b_high, a_high, b_high, a_low, b_low], axis=1)
        out = jnp.dot(wide, right_ref[...], preferred_element_type=jnp.float32)
        return out[:, :n], out[:, n:]

    padded[:, :n, :] = jnp.zeros((2, n, 2 * n), jnp.float32)
    padded[:, 2 * n :, :] = jnp.zeros((2, n, 2 * n), jnp.float32)
    grad[...] = jnp.zeros(grad.shape, jnp.float32)
    partial[...] = jnp.zeros(partial.shape, jnp.float32)

    def visit(p, carry):
        row_at = rows_ref[p] - tile * n
        col_at = cols_ref[p] - col * n
        shift = lax.rem(2 * n - col_at, 2 * n)
        alive = jnp.where(p < counts_ref[0], 1.0, 0.0).astype(jnp.float32)
        aligned = pl.multiple_of(row_at // 8 * 8, 8)
        inner = row_at % 8
        sublane = lax.broadcasted_iota(jnp.int32, (1, 8, 2 * n), 1)
        for k in range(2):
            rows = region[k, pl.ds(aligned, n + 8), :].reshape(n // 8 + 1, 8, 2 * n)
            rows = pltpu.roll(rows, lax.rem(8 - inner, 8), 1)
            rows = jnp.where(sublane < 8 - inner, rows[:-1], rows[1:]).reshape(n, 2 * n)
            patch_ref[k] = pltpu.roll(rows, shift, 1)[:, :n]
        obj_r, obj_i = patch_ref[0], patch_ref[1]
        probe_r, probe_i = probe[0], probe[1]
        wave_r, wave_i = propagate(
            probe_r * obj_r - probe_i * obj_i, probe_r * obj_i + probe_i * obj_r
        )
        excess = (wave_r * wave_r + wave_i * wave_i - patterns_ref[p]) * alive
        back_r, back_m = propagate(excess * wave_r, -(excess * wave_i))
        obj_r, obj_i = patch_ref[0], patch_ref[1]
        probe_r, probe_i = probe[0], probe[1]
        partial[0] += obj_r * back_r - obj_i * back_m
        partial[1] += -(obj_r * back_m) - obj_i * back_r
        partial[2] += alive * (obj_r * obj_r + obj_i * obj_i)
        terms = (probe_r * back_r - probe_i * back_m, -(probe_r * back_m) - probe_i * back_r)
        for k in range(2):
            wide = jnp.concatenate([terms[k], jnp.zeros((n, n), jnp.float32)], axis=1)
            wide = pltpu.roll(wide, col_at, 1).reshape(n // 8, 8, 2 * n)
            wide = pltpu.roll(wide, inner, 1)
            empty = jnp.zeros((1, 8, 2 * n), jnp.float32)
            after, before = jnp.concatenate([wide, empty], 0), jnp.concatenate([empty, wide], 0)
            wide = jnp.where(sublane < inner, before, after).reshape(n + 8, 2 * n)
            padded[k, n : 2 * n + 8, :] = wide
            grad[k] += padded[k, pl.ds(pl.multiple_of(n - aligned, 8), 2 * n), :]
        return carry

    lax.fori_loop(0, slots, visit, 0)


def exchange_first(
    sizes, fresnel_ref, object_ref, cosine_ref, sine_ref, region, left_ref, right_ref, halo_send, halo_recv
):
    n_row, n_col, n_sub = sizes
    n = region.shape[1] // 2
    step_rows = n // CHUNKS
    row, col, sub = lax.axis_index("row"), lax.axis_index("col"), lax.axis_index("sub")
    tile = row * n_sub + sub
    n_tile = n_row * n_sub
    has_up, has_down = tile > 0, tile < n_tile - 1
    has_left, has_right = col > 0, col < n_col - 1
    up = {"row": (tile + n_tile - 1) % n_tile // n_sub, "sub": (tile + n_tile - 1) % n_tile % n_sub}
    down = {"row": (tile + 1) % n_tile // n_sub, "sub": (tile + 1) % n_tile % n_sub}
    left = {"col": (col + n_col - 1) % n_col}
    right = {"col": (col + 1) % n_col}

    barrier = pltpu.get_barrier_semaphore()

    def greet(where):
        pl.semaphore_signal(barrier, inc=1, device_id=where, device_id_type=MESH)

    for d in range(1, n_row):
        greet({"row": (row + d) % n_row})
    for d in range(1, n_col):
        greet({"col": (col + d) % n_col})
    for d in range(1, n_sub):
        greet({"sub": (sub + d) % n_sub})
    cross_up = (sub == 0) & (row > 0)
    cross_down = (sub == n_sub - 1) & (row < n_row - 1)
    pl.when(cross_up)(lambda: greet(up))
    pl.when(cross_down)(lambda: greet(down))
    crossing = cross_up.astype(jnp.int32) + cross_down.astype(jnp.int32)
    pl.semaphore_wait(barrier, n_row + n_col + n_sub - 3 + crossing)

    def remote(src, dst, send, recv, where):
        return pltpu.make_async_remote_copy(
            src_ref=src, dst_ref=dst, send_sem=send, recv_sem=recv, device_id=where, device_id_type=MESH
        )

    def halo(kind, q):
        at = pl.ds(q * step_rows, step_rows)
        below = pl.ds(n + q * step_rows, step_rows)
        own, far = pl.ds(0, n), pl.ds(n, n)
        src, dst, where = (
            (region.at[:, at, own], region.at[:, at, far], left),
            (region.at[:, at, own], region.at[:, below, own], up),
            (region.at[:, at, far], region.at[:, below, far], up),
        )[kind]
        return remote(src, dst, halo_send.at[kind, q], halo_recv.at[kind, q], where)

    halo_out = (has_left, has_up, has_up & has_right)
    halo_in = (has_right, has_down, has_down & has_right)

    def when_start(cond, copy):
        pl.when(cond)(lambda: copy.start())

    def when_recv(cond, copy):
        pl.when(cond)(lambda: copy.wait_recv())

    def clear_edges():
        @pl.when(~has_right)
        def _():
            region[:, :, n:] = jnp.zeros((2, 2 * n, n), jnp.float32)

        @pl.when(~has_down)
        def _():
            region[:, n:, :] = jnp.zeros((2, n, 2 * n), jnp.float32)

    clear_edges()
    region[:, :n, :n] = object_ref[...]
    for q in range(CHUNKS):
        when_start(halo_out[0], halo(0, q))
        when_start(halo_out[1], halo(1, q))
    build_propagator(n, fresnel_ref, cosine_ref, sine_ref, left_ref, right_ref)
    for q in range(CHUNKS):
        when_recv(halo_in[0], halo(0, q))
        when_start(halo_out[2], halo(2, q))
    for q in range(CHUNKS):
        when_recv(halo_in[1], halo(1, q))
        when_recv(halo_in[2], halo(2, q))
    for q in range(CHUNKS):
        for kind in range(3):
            pl.when(halo_out[kind])(lambda copy=halo(kind, q): copy.wait_send())


def exchange_next(
    sizes,
    last,
    object_step_ref,
    probe_step_ref,
    old_region,
    probe,
    grad,
    partial,
    target,
    probe_next,
    far_sum,
    own_sum,
    total,
    from_up,
    from_corner,
    from_left,
    from_sub,
    from_col,
    from_row,
    halo_send,
    halo_recv,
    spill_send,
    spill_recv,
    sub_send,
    sub_recv,
    col_send,
    col_recv,
    row_send,
    row_recv,
):
    region = target if not last else old_region
    n_row, n_col, n_sub = sizes
    n = region.shape[1] // 2
    step_rows = n // CHUNKS
    row, col, sub = lax.axis_index("row"), lax.axis_index("col"), lax.axis_index("sub")
    tile = row * n_sub + sub
    n_tile = n_row * n_sub
    has_up, has_down = tile > 0, tile < n_tile - 1
    has_left, has_right = col > 0, col < n_col - 1
    up = {"row": (tile + n_tile - 1) % n_tile // n_sub, "sub": (tile + n_tile - 1) % n_tile % n_sub}
    down = {"row": (tile + 1) % n_tile // n_sub, "sub": (tile + 1) % n_tile % n_sub}
    left = {"col": (col + n_col - 1) % n_col}
    right = {"col": (col + 1) % n_col}

    barrier = pltpu.get_barrier_semaphore()

    def greet(where):
        pl.semaphore_signal(barrier, inc=1, device_id=where, device_id_type=MESH)

    for d in range(1, n_row):
        greet({"row": (row + d) % n_row})
    for d in range(1, n_col):
        greet({"col": (col + d) % n_col})
    for d in range(1, n_sub):
        greet({"sub": (sub + d) % n_sub})
    cross_up = (sub == 0) & (row > 0)
    cross_down = (sub == n_sub - 1) & (row < n_row - 1)
    pl.when(cross_up)(lambda: greet(up))
    pl.when(cross_down)(lambda: greet(down))
    crossing = cross_up.astype(jnp.int32) + cross_down.astype(jnp.int32)
    pl.semaphore_wait(barrier, n_row + n_col + n_sub - 3 + crossing)

    def remote(src, dst, send, recv, where):
        return pltpu.make_async_remote_copy(
            src_ref=src, dst_ref=dst, send_sem=send, recv_sem=recv, device_id=where, device_id_type=MESH
        )

    def halo(kind, q):
        at = pl.ds(q * step_rows, step_rows)
        below = pl.ds(n + q * step_rows, step_rows)
        own, far = pl.ds(0, n), pl.ds(n, n)
        src, dst, where = (
            (region.at[:, at, own], region.at[:, at, far], left),
            (region.at[:, at, own], region.at[:, below, own], up),
            (region.at[:, at, far], region.at[:, below, far], up),
        )[kind]
        return remote(src, dst, halo_send.at[kind, q], halo_recv.at[kind, q], where)

    halo_out = (has_left, has_up, has_up & has_right)
    halo_in = (has_right, has_down, has_down & has_right)

    def spill(kind, q):
        at = pl.ds(q * step_rows, step_rows)
        below = pl.ds(n + q * step_rows, step_rows)
        own, far = pl.ds(0, n), pl.ds(n, n)
        src, dst, where = (
            (far_sum.at[:, at, :], from_left.at[:, at, :], right),
            (grad.at[:, below, own], from_up.at[:, at, :], down),
            (grad.at[:, below, far], from_corner.at[:, at, :], down),
        )[kind]
        return remote(src, dst, spill_send.at[kind, q], spill_recv.at[kind, q], where)

    spill_out = (has_right, has_down, has_down & has_right)
    spill_in = (has_left, has_up, has_up & has_right)

    def when_start(cond, copy):
        pl.when(cond)(lambda: copy.start())

    def when_recv(cond, copy):
        pl.when(cond)(lambda: copy.wait_recv())

    def clear_edges():
        @pl.when(~has_right)
        def _():
            region[:, :, n:] = jnp.zeros((2, 2 * n, n), jnp.float32)

        @pl.when(~has_down)
        def _():
            region[:, n:, :] = jnp.zeros((2, n, 2 * n), jnp.float32)

    sub_rows = n // n_sub
    col_rows = sub_rows // n_col
    pieces = min(n_row, col_rows // 8)
    row_rows = col_rows // pieces
    sub_base = sub * sub_rows
    col_base = sub_base + col * col_rows
    row_base = col_base + row * row_rows
    owns = row < pieces

    def span(start, length):
        return pl.ds(pl.multiple_of(start, 8), length)

    def scatter_sub(d):
        to = (sub + d) % n_sub
        return remote(
            partial.at[:, span(to * sub_rows, sub_rows), :], from_sub.at[d - 1],
            sub_send.at[0, d - 1], sub_recv.at[0, d - 1], {"sub": to},
        )

    def scatter_col(d):
        to = (col + d) % n_col
        return remote(
            total.at[:, span(to * col_rows, col_rows), :], from_col.at[d - 1],
            col_send.at[0, d - 1], col_recv.at[0, d - 1], {"col": to},
        )

    def scatter_row(d):
        to = (row + d) % n_row
        return remote(
            total.at[:, span(col * col_rows + jnp.minimum(to, pieces - 1) * row_rows, row_rows), :],
            from_row.at[d - 1],
            row_send.at[0, d - 1], row_recv.at[0, d - 1], {"row": to},
        )

    def gather(axis, d):
        me, count, base, length, send, recv = {
            "row": (row, n_row, row_base, row_rows, row_send, row_recv),
            "col": (col, n_col, col_base, col_rows, col_send, col_recv),
            "sub": (sub, n_sub, sub_base, sub_rows, sub_send, sub_recv),
        }[axis]
        part = probe_next.at[:, span(base, length), :]
        return remote(part, part, send.at[1, d - 1], recv.at[1, d - 1], {axis: (me + d) % count})

    for d in range(1, n_sub):
        scatter_sub(d).start()
    for q in range(CHUNKS):
        when_start(spill_out[2], spill(2, q))
    for q in range(CHUNKS):
        when_start(spill_out[1], spill(1, q))
    if not last:
        clear_edges()
    far_sum[...] = grad[:, :n, n:]
    own_sum[...] = grad[:, :n, :n]
    peak = probe[0] * probe[0] + probe[1] * probe[1]
    peak = jnp.max(jnp.max(peak, axis=0, keepdims=True), axis=1, keepdims=True)
    scale = object_step_ref[0] / (peak + 1e-6)

    total[...] = partial[:, span(sub_base, sub_rows), :]
    for d in range(1, n_sub):
        scatter_sub(d).wait_recv()
        total[...] += from_sub[d - 1]
    for d in range(1, n_col):
        scatter_col(d).start()

    for q in range(CHUNKS):
        at = slice(q * step_rows, (q + 1) * step_rows)

        @pl.when(spill_in[2])
        def _():
            spill(2, q).wait_recv()
            far_sum[:, at, :] += from_corner[:, at, :]

        when_start(spill_out[0], spill(0, q))

    mine = span(col * col_rows, col_rows)
    for d in range(1, n_col):
        scatter_col(d).wait_recv()
        total[:, mine, :] += from_col[d - 1]
    for d in range(1, n_row):
        copy = scatter_row(d)
        if pieces == n_row:
            copy.start()
        else:
            when_start((row + d) % n_row < pieces, copy)

    for q in range(CHUNKS):
        at = slice(q * step_rows, (q + 1) * step_rows)

        @pl.when(spill_in[1])
        def _():
            spill(1, q).wait_recv()
            own_sum[:, at, :] += from_up[:, at, :]

        @pl.when(spill_in[0])
        def _():
            spill(0, q).wait_recv()
            own_sum[:, at, :] += from_left[:, at, :]

        fresh = old_region[:, at, :n] - scale * own_sum[:, at, :]
        if last:
            target[:, at, :] = fresh
        else:
            region[:, at, :n] = fresh
            when_start(halo_out[0], halo(0, q))
            when_start(halo_out[1], halo(1, q))

    def finish_piece():
        mine = span(row_base, row_rows)
        sums = total[:, span(col * col_rows + row * row_rows, row_rows), :]
        for d in range(1, n_row):
            scatter_row(d).wait_recv()
            sums = sums + from_row[d - 1]
        for k in range(2):
            probe_next[k, mine, :] = probe[k, mine, :] - probe_step_ref[0] * sums[k] / (sums[2] + 1.0)
        for d in range(1, n_row):
            gather("row", d).start()

    if pieces == n_row:
        finish_piece()
    else:
        pl.when(owns)(finish_piece)
    if not last:
        for q in range(CHUNKS):
            when_recv(halo_in[0], halo(0, q))
            when_start(halo_out[2], halo(2, q))
    for d in range(1, n_row):
        copy = gather("row", d)
        if pieces == n_row:
            copy.wait_recv()
        else:
            when_recv((row + n_row - d) % n_row < pieces, copy)
    for axis, count in (("col", n_col), ("sub", n_sub)):
        for d in range(1, count):
            gather(axis, d).start()
        for d in range(1, count):
            gather(axis, d).wait_recv()
    if not last:
        for q in range(CHUNKS):
            when_recv(halo_in[1], halo(1, q))
            when_recv(halo_in[2], halo(2, q))

    for q in range(CHUNKS):
        for kind in range(3):
            pl.when(spill_out[kind])(lambda copy=spill(kind, q): copy.wait_send())
            if not last:
                pl.when(halo_out[kind])(lambda copy=halo(kind, q): copy.wait_send())
    for d in range(1, n_sub):
        scatter_sub(d).wait_send()
        gather("sub", d).wait_send()
    for d in range(1, n_col):
        scatter_col(d).wait_send()
        gather("col", d).wait_send()
    for d in range(1, n_row):
        for cond, copy in (((row + d) % n_row < pieces, scatter_row(d)), (owns, gather("row", d))):
            if pieces == n_row:
                copy.wait_send()
            else:
                pl.when(cond)(lambda copy=copy: copy.wait_send())


def solution(mesh):
    n_row, n_col, n_sub = mesh.shape["row"], mesh.shape["col"], mesh.shape["sub"]

    def local(
        object_field, probe_field, patterns, offset_rows, offset_cols, counts, fresnel, object_step, probe_step
    ):
        n = probe_field.shape[1]
        index = np.arange(n)
        angles = 2.0 * np.pi / n * (index[:, None] * index[None, :] % n)
        cosine = np.cos(angles).astype(np.float32)
        sine = np.sin(angles).astype(np.float32)
        sub_rows = n // n_sub
        col_rows = sub_rows // n_col
        row_rows = col_rows // min(n_row, col_rows // 8)
        f32 = jnp.float32
        dma = pltpu.SemaphoreType.DMA
        smem = pl.BlockSpec(memory_space=pltpu.SMEM)
        vmem = pl.BlockSpec(memory_space=pltpu.VMEM)
        sizes = (n_row, n_col, n_sub)
        region_shape = jax.ShapeDtypeStruct((2, 2 * n, 2 * n), f32)
        tile_shape = jax.ShapeDtypeStruct((2, n, n), f32)
        tile_scratch = pltpu.VMEM((2, n, n), f32)
        limit = 24 * 1024 * 1024
        copies = [dma((3, CHUNKS)), dma((3, CHUNKS))]

        region, left, right = pl.pallas_call(
            functools.partial(exchange_first, sizes),
            out_shape=(
                region_shape,
                jax.ShapeDtypeStruct((2 * n, 6 * n), jnp.bfloat16),
                jax.ShapeDtypeStruct((6 * n, 2 * n), jnp.bfloat16),
            ),
            in_specs=[smem, vmem, vmem, vmem],
            out_specs=(vmem, vmem, vmem),
            scratch_shapes=copies,
            compiler_params=pltpu.CompilerParams(
                collective_id=0, has_side_effects=True, vmem_limit_bytes=limit
            ),
        )(fresnel, object_field, jnp.asarray(cosine), jnp.asarray(sine))

        probe = probe_field
        for it in range(ITERS):
            last = it == ITERS - 1
            grad, partial = pl.pallas_call(
                functools.partial(gradients, sizes),
                out_shape=(region_shape, jax.ShapeDtypeStruct((3, n, n), f32)),
                in_specs=[smem] * 3 + [vmem] * 5,
                out_specs=(vmem, vmem),
                scratch_shapes=[
                    pltpu.VMEM((2, 3 * n, 2 * n), f32),
                    pltpu.VMEM((6 * n, n), jnp.bfloat16),
                    tile_scratch,
                ],
                compiler_params=pltpu.CompilerParams(vmem_limit_bytes=limit),
            )(offset_rows, offset_cols, counts, region, probe, patterns, left, right)
            region, probe = pl.pallas_call(
                functools.partial(exchange_next, sizes, last),
                out_shape=(tile_shape if last else region_shape, tile_shape),
                in_specs=[smem] * 2 + [vmem] * 4,
                out_specs=(vmem, vmem),
                scratch_shapes=[
                    tile_scratch,
                    tile_scratch,
                    pltpu.VMEM((3, sub_rows, n), f32),
                    tile_scratch,
                    tile_scratch,
                    tile_scratch,
                    pltpu.VMEM((n_sub - 1, 3, sub_rows, n), f32),
                    pltpu.VMEM((n_col - 1, 3, col_rows, n), f32),
                    pltpu.VMEM((n_row - 1, 3, row_rows, n), f32),
                ]
                + copies
                + copies
                + [dma((2, count - 1)) for count in (n_sub, n_sub, n_col, n_col, n_row, n_row)],
                compiler_params=pltpu.CompilerParams(
                    collective_id=1 + it, has_side_effects=True, vmem_limit_bytes=limit
                ),
            )(object_step, probe_step, region, probe, grad, partial)
        return region, probe

    owners = ("groups", "row", "col", "sub")
    tiled = P(None, ("groups", "row", "sub"), "col")
    probes = P("groups", None, None)
    return jax.shard_map(
        local,
        mesh=mesh,
        in_specs=(tiled, probes, P(owners, None, None), P(owners), P(owners), P(owners), P(), P(), P()),
        out_specs=(tiled, probes),
        check_vma=False,
    )
```

```python
import functools
import math

import jax
import jax.numpy as jnp
from jax import lax
from jax.experimental import pallas as pl
from jax.experimental.pallas import tpu as pltpu
from jax.sharding import PartitionSpec as P

ITERS = 2
CHUNKS = 4
HALVES = 2
HIGHEST = lax.Precision.HIGHEST
MESH = pl.DeviceIdType.MESH


def split(value):
    high = value.astype(jnp.bfloat16)
    return high, (value - high.astype(jnp.float32)).astype(jnp.bfloat16)


def build_propagator(n, fresnel_ref, left_ref, right_ref):
    freq = lax.broadcasted_iota(jnp.int32, (8, n), 1)
    freq = jnp.where(freq < n // 2, freq, freq - n).astype(jnp.float32)
    phases = -math.pi / n * fresnel_ref[0] * freq * freq
    trans_r = jnp.cos(phases)[0:1]
    trans_i = jnp.sin(phases)[0:1]
    product = lax.broadcasted_iota(jnp.int32, (n, n), 0) * lax.broadcasted_iota(jnp.int32, (n, n), 1)
    angles = 2.0 * math.pi / n * lax.rem(product, n).astype(jnp.float32)
    cosine = jnp.cos(angles)
    sine = jnp.sin(angles)
    half_r = (cosine * trans_r - sine * trans_i) * (1.0 / n)
    half_i = (cosine * trans_i + sine * trans_r) * (1.0 / n)

    def exact(a, b):
        return jnp.dot(a, b, precision=HIGHEST, preferred_element_type=jnp.float32)

    kern_r = exact(half_r, cosine) + exact(half_i, sine)
    kern_i = exact(half_i, cosine) - exact(half_r, sine)
    r_high, r_low = split(kern_r)
    i_high, i_low = split(kern_i)
    for part, (r_half, i_half) in enumerate(((r_high, i_high), (r_low, i_low), (r_high, i_high))):
        base = part * 2 * n
        left_ref[:n, base : base + n] = r_half
        left_ref[:n, base + n : base + 2 * n] = -i_half
        left_ref[n:, base : base + n] = i_half
        left_ref[n:, base + n : base + 2 * n] = r_half
        right_ref[part * n : (part + 1) * n, :n] = r_half
        right_ref[part * n : (part + 1) * n, n:] = i_half


def gradients(
    sizes,
    rows_ref,
    cols_ref,
    counts_ref,
    region,
    probe,
    patterns_ref,
    left_ref,
    right_ref,
    grad,
    partial,
    padded,
    stacked,
    patch_ref,
):
    n_sub = sizes[2]
    slots, n = patterns_ref.shape[0], patterns_ref.shape[1]
    tile = lax.axis_index("row") * n_sub + lax.axis_index("sub")
    col = lax.axis_index("col")

    def propagate(stacked, x_r, x_i):
        for k, value in enumerate((x_r, x_i)):
            high, low = split(value)
            stacked[k * n : (k + 1) * n, :] = high
            stacked[(k + 2) * n : (k + 3) * n, :] = high
            stacked[(k + 4) * n : (k + 5) * n, :] = low
        mid = jnp.dot(left_ref[...], stacked[...], preferred_element_type=jnp.float32)
        high, low = split(mid)
        wide = jnp.concatenate([high, high, low], axis=1)
        out = jnp.dot(wide, right_ref[...], preferred_element_type=jnp.float32)
        return out[:n, :n] - out[n:, n:], out[:n, n:] + out[n:, :n]

    padded[:, :n, :] = jnp.zeros((padded.shape[0], n, 2 * n), jnp.float32)
    padded[:, 2 * n :, :] = jnp.zeros((padded.shape[0], n, 2 * n), jnp.float32)
    grad[...] = jnp.zeros(grad.shape, jnp.float32)
    partial[...] = jnp.zeros(partial.shape, jnp.float32)

    def visit(p):
        row_at = rows_ref[p] - tile * n
        col_at = cols_ref[p] - col * n
        shift = lax.rem(2 * n - col_at, 2 * n)
        alive = jnp.where(p < counts_ref[0], 1.0, 0.0).astype(jnp.float32)
        aligned = pl.multiple_of(row_at // 8 * 8, 8)
        inner = row_at % 8
        sublane = lax.broadcasted_iota(jnp.int32, (1, 8, 2 * n), 1)
        for k in range(2):
            rows = region[k, pl.ds(aligned, n + 8), :].reshape(n // 8 + 1, 8, 2 * n)
            rows = pltpu.roll(rows, lax.rem(8 - inner, 8), 1)
            rows = jnp.where(sublane < 8 - inner, rows[:-1], rows[1:]).reshape(n, 2 * n)
            patch_ref[2 * p + k] = pltpu.roll(rows, shift, 1)[:, :n]
        obj_r, obj_i = patch_ref[2 * p], patch_ref[2 * p + 1]
        probe_r, probe_i = probe[0], probe[1]
        wave_r, wave_i = propagate(
            stacked.at[2 * p], probe_r * obj_r - probe_i * obj_i, probe_r * obj_i + probe_i * obj_r
        )
        excess = (wave_r * wave_r + wave_i * wave_i - patterns_ref[p]) * alive
        back_r, back_m = propagate(stacked.at[2 * p + 1], excess * wave_r, -(excess * wave_i))
        obj_r, obj_i = patch_ref[2 * p], patch_ref[2 * p + 1]
        probe_r, probe_i = probe[0], probe[1]
        partial[0] += obj_r * back_r - obj_i * back_m
        partial[1] += -(obj_r * back_m) - obj_i * back_r
        partial[2] += alive * (obj_r * obj_r + obj_i * obj_i)
        terms = (probe_r * back_r - probe_i * back_m, -(probe_r * back_m) - probe_i * back_r)
        for k in range(2):
            wide = jnp.concatenate([terms[k], jnp.zeros((n, n), jnp.float32)], axis=1)
            wide = pltpu.roll(wide, col_at, 1).reshape(n // 8, 8, 2 * n)
            wide = pltpu.roll(wide, inner, 1)
            empty = jnp.zeros((1, 8, 2 * n), jnp.float32)
            after, before = jnp.concatenate([wide, empty], 0), jnp.concatenate([empty, wide], 0)
            wide = jnp.where(sublane < inner, before, after).reshape(n + 8, 2 * n)
            padded[2 * p + k, n : 2 * n + 8, :] = wide
            grad[k] += padded[2 * p + k, pl.ds(pl.multiple_of(n - aligned, 8), 2 * n), :]

    for p in range(slots):
        visit(p)


def exchange_first(
    sizes, fresnel_ref, object_ref, region, left_ref, right_ref, halo_send, halo_recv
):
    n_row, n_col, n_sub = sizes
    n = region.shape[1] // 2
    step_rows = n // CHUNKS
    row, col, sub = lax.axis_index("row"), lax.axis_index("col"), lax.axis_index("sub")
    tile = row * n_sub + sub
    n_tile = n_row * n_sub
    has_up, has_down = tile > 0, tile < n_tile - 1
    has_left, has_right = col > 0, col < n_col - 1
    up = {"row": (tile + n_tile - 1) % n_tile // n_sub, "sub": (tile + n_tile - 1) % n_tile % n_sub}
    down = {"row": (tile + 1) % n_tile // n_sub, "sub": (tile + 1) % n_tile % n_sub}
    left = {"col": (col + n_col - 1) % n_col}
    right = {"col": (col + 1) % n_col}

    barrier = pltpu.get_barrier_semaphore()

    def greet(where):
        pl.semaphore_signal(barrier, inc=1, device_id=where, device_id_type=MESH)

    for d in range(1, n_row):
        greet({"row": (row + d) % n_row})
    for d in range(1, n_col):
        greet({"col": (col + d) % n_col})
    for d in range(1, n_sub):
        greet({"sub": (sub + d) % n_sub})
    cross_up = (sub == 0) & (row > 0)
    cross_down = (sub == n_sub - 1) & (row < n_row - 1)
    pl.when(cross_up)(lambda: greet(up))
    pl.when(cross_down)(lambda: greet(down))
    crossing = cross_up.astype(jnp.int32) + cross_down.astype(jnp.int32)
    pl.semaphore_wait(barrier, n_row + n_col + n_sub - 3 + crossing)

    def remote(src, dst, send, recv, where):
        return pltpu.make_async_remote_copy(
            src_ref=src, dst_ref=dst, send_sem=send, recv_sem=recv, device_id=where, device_id_type=MESH
        )

    def halo(kind, q):
        at = pl.ds(q * step_rows, step_rows)
        below = pl.ds(n + q * step_rows, step_rows)
        own, far = pl.ds(0, n), pl.ds(n, n)
        src, dst, where = (
            (region.at[:, at, own], region.at[:, at, far], left),
            (region.at[:, at, own], region.at[:, below, own], up),
            (region.at[:, at, far], region.at[:, below, far], up),
        )[kind]
        return remote(src, dst, halo_send.at[kind, q], halo_recv.at[kind, q], where)

    halo_out = (has_left, has_up, has_up & has_right)
    halo_in = (has_right, has_down, has_down & has_right)

    def when_start(cond, copy):
        pl.when(cond)(lambda: copy.start())

    def when_recv(cond, copy):
        pl.when(cond)(lambda: copy.wait_recv())

    def clear_edges():
        @pl.when(~has_right)
        def _():
            region[:, :, n:] = jnp.zeros((2, 2 * n, n), jnp.float32)

        @pl.when(~has_down)
        def _():
            region[:, n:, :] = jnp.zeros((2, n, 2 * n), jnp.float32)

    region[:, :n, :n] = object_ref[...]
    for q in range(CHUNKS):
        when_start(halo_out[0], halo(0, q))
        when_start(halo_out[1], halo(1, q))
    clear_edges()
    build_propagator(n, fresnel_ref, left_ref, right_ref)
    for q in range(CHUNKS):
        when_recv(halo_in[0], halo(0, q))
        when_start(halo_out[2], halo(2, q))
    for q in range(CHUNKS):
        when_recv(halo_in[1], halo(1, q))
        when_recv(halo_in[2], halo(2, q))
    for q in range(CHUNKS):
        for kind in range(3):
            pl.when(halo_out[kind])(lambda copy=halo(kind, q): copy.wait_send())


def exchange_next(
    sizes,
    last,
    object_step_ref,
    probe_step_ref,
    old_region,
    probe,
    grad,
    partial,
    target,
    probe_next,
    far_sum,
    own_sum,
    total,
    from_up,
    from_corner,
    from_left,
    from_sub,
    from_col,
    from_row,
    halo_send,
    halo_recv,
    spill_send,
    spill_recv,
    sub_send,
    sub_recv,
    col_send,
    col_recv,
    row_send,
    row_recv,
):
    region = target if not last else old_region
    n_row, n_col, n_sub = sizes
    n = region.shape[1] // 2
    step_rows = n // CHUNKS
    row, col, sub = lax.axis_index("row"), lax.axis_index("col"), lax.axis_index("sub")
    tile = row * n_sub + sub
    n_tile = n_row * n_sub
    has_up, has_down = tile > 0, tile < n_tile - 1
    has_left, has_right = col > 0, col < n_col - 1
    up = {"row": (tile + n_tile - 1) % n_tile // n_sub, "sub": (tile + n_tile - 1) % n_tile % n_sub}
    down = {"row": (tile + 1) % n_tile // n_sub, "sub": (tile + 1) % n_tile % n_sub}
    left = {"col": (col + n_col - 1) % n_col}
    right = {"col": (col + 1) % n_col}

    barrier = pltpu.get_barrier_semaphore()

    def greet(where):
        pl.semaphore_signal(barrier, inc=1, device_id=where, device_id_type=MESH)

    for d in range(1, n_row):
        greet({"row": (row + d) % n_row})
    for d in range(1, n_col):
        greet({"col": (col + d) % n_col})
    for d in range(1, n_sub):
        greet({"sub": (sub + d) % n_sub})
    cross_up = (sub == 0) & (row > 0)
    cross_down = (sub == n_sub - 1) & (row < n_row - 1)
    pl.when(cross_up)(lambda: greet(up))
    pl.when(cross_down)(lambda: greet(down))
    crossing = cross_up.astype(jnp.int32) + cross_down.astype(jnp.int32)
    pl.semaphore_wait(barrier, n_row + n_col + n_sub - 3 + crossing)

    def remote(src, dst, send, recv, where):
        return pltpu.make_async_remote_copy(
            src_ref=src, dst_ref=dst, send_sem=send, recv_sem=recv, device_id=where, device_id_type=MESH
        )

    def halo(kind, q):
        at = pl.ds(q * step_rows, step_rows)
        below = pl.ds(n + q * step_rows, step_rows)
        own, far = pl.ds(0, n), pl.ds(n, n)
        src, dst, where = (
            (region.at[:, at, own], region.at[:, at, far], left),
            (region.at[:, at, own], region.at[:, below, own], up),
            (region.at[:, at, far], region.at[:, below, far], up),
        )[kind]
        return remote(src, dst, halo_send.at[kind, q], halo_recv.at[kind, q], where)

    halo_out = (has_left, has_up, has_up & has_right)
    halo_in = (has_right, has_down, has_down & has_right)

    def spill(kind, q):
        at = pl.ds(q * step_rows, step_rows)
        below = pl.ds(n + q * step_rows, step_rows)
        own, far = pl.ds(0, n), pl.ds(n, n)
        src, dst, where = (
            (far_sum.at[:, at, :], from_left.at[:, at, :], right),
            (grad.at[:, below, own], from_up.at[:, at, :], down),
            (grad.at[:, below, far], from_corner.at[:, at, :], down),
        )[kind]
        return remote(src, dst, spill_send.at[kind, q], spill_recv.at[kind, q], where)

    spill_out = (has_right, has_down, has_down & has_right)
    spill_in = (has_left, has_up, has_up & has_right)

    def when_start(cond, copy):
        pl.when(cond)(lambda: copy.start())

    def when_recv(cond, copy):
        pl.when(cond)(lambda: copy.wait_recv())

    def clear_edges():
        @pl.when(~has_right)
        def _():
            region[:, :, n:] = jnp.zeros((2, 2 * n, n), jnp.float32)

        @pl.when(~has_down)
        def _():
            region[:, n:, :] = jnp.zeros((2, n, 2 * n), jnp.float32)

    sub_rows = n // HALVES // n_sub
    col_rows = sub_rows // n_col
    pieces = min(n_row, col_rows // 8)
    row_rows = col_rows // pieces
    sub_base = [h * (n // HALVES) + sub * sub_rows for h in range(HALVES)]
    col_base = [base + col * col_rows for base in sub_base]
    row_base = [base + row * row_rows for base in col_base]
    owns = row < pieces

    def span(start, length):
        return pl.ds(pl.multiple_of(start, 8), length)

    def scatter_sub(h, d):
        to = (sub + d) % n_sub
        return remote(
            partial.at[:, span(h * (n // HALVES) + to * sub_rows, sub_rows), :], from_sub.at[h, d - 1],
            sub_send.at[h, 0, d - 1], sub_recv.at[h, 0, d - 1], {"sub": to},
        )

    def scatter_col(h, d):
        to = (col + d) % n_col
        return remote(
            total.at[h, :, span(to * col_rows, col_rows), :], from_col.at[h, d - 1],
            col_send.at[h, 0, d - 1], col_recv.at[h, 0, d - 1], {"col": to},
        )

    def scatter_row(h, d):
        to = (row + d) % n_row
        return remote(
            total.at[h, :, span(col * col_rows + jnp.minimum(to, pieces - 1) * row_rows, row_rows), :],
            from_row.at[h, d - 1],
            row_send.at[h, 0, d - 1], row_recv.at[h, 0, d - 1], {"row": to},
        )

    def gather(h, axis, d):
        me, count, base, length, send, recv = {
            "row": (row, n_row, row_base[h], row_rows, row_send, row_recv),
            "col": (col, n_col, col_base[h], col_rows, col_send, col_recv),
            "sub": (sub, n_sub, sub_base[h], sub_rows, sub_send, sub_recv),
        }[axis]
        part = probe_next.at[:, span(base, length), :]
        return remote(part, part, send.at[h, 1, d - 1], recv.at[h, 1, d - 1], {axis: (me + d) % count})

    halves = range(HALVES)
    for h in halves:
        for d in range(1, n_sub):
            scatter_sub(h, d).start()
    for q in range(CHUNKS):
        when_start(spill_out[2], spill(2, q))
    far_sum[...] = grad[:, :n, n:]
    mine = span(col * col_rows, col_rows)
    for h in halves:
        total[h] = partial[:, span(sub_base[h], sub_rows), :]
        for d in range(1, n_sub):
            scatter_sub(h, d).wait_recv()
            total[h] += from_sub[h, d - 1]
        for d in range(1, n_col):
            scatter_col(h, d).start()
    ahead = 1 if last else CHUNKS
    for q in range(ahead):
        when_start(spill_out[1], spill(1, q))
    own_sum[...] = grad[:, :n, :n]
    if not last:
        clear_edges()
    peak = probe[0] * probe[0] + probe[1] * probe[1]
    peak = jnp.max(jnp.max(peak, axis=0, keepdims=True), axis=1, keepdims=True)
    scale = object_step_ref[0] / (peak + 1e-6)

    def pass_right(q):
        at = slice(q * step_rows, (q + 1) * step_rows)

        @pl.when(spill_in[2])
        def _():
            spill(2, q).wait_recv()
            far_sum[:, at, :] += from_corner[:, at, :]

        when_start(spill_out[0], spill(0, q))

    for h in halves:
        for d in range(1, n_col):
            scatter_col(h, d).wait_recv()
            total[h, :, mine, :] += from_col[h, d - 1]
        for d in range(1, n_row):
            copy = scatter_row(h, d)
            if pieces == n_row:
                copy.start()
            else:
                when_start((row + d) % n_row < pieces, copy)
        pass_right(h)
    for q in range(ahead, CHUNKS):
        when_start(spill_out[1], spill(1, q))
    for q in range(HALVES, CHUNKS):
        pass_right(q)

    def finish_piece(h):
        mine = span(row_base[h], row_rows)
        sums = total[h, :, span(col * col_rows + row * row_rows, row_rows), :]
        for d in range(1, n_row):
            scatter_row(h, d).wait_recv()
            sums = sums + from_row[h, d - 1]
        for k in range(2):
            probe_next[k, mine, :] = probe[k, mine, :] - probe_step_ref[0] * sums[k] / (sums[2] + 1.0)
        for d in range(1, n_row):
            gather(h, "row", d).start()

    def update(q):
        at = slice(q * step_rows, (q + 1) * step_rows)

        @pl.when(spill_in[1])
        def _():
            spill(1, q).wait_recv()
            own_sum[:, at, :] += from_up[:, at, :]

        @pl.when(spill_in[0])
        def _():
            spill(0, q).wait_recv()
            own_sum[:, at, :] += from_left[:, at, :]

        fresh = old_region[:, at, :n] - scale * own_sum[:, at, :]
        if last:
            target[:, at, :] = fresh
        else:
            region[:, at, :n] = fresh
            when_start(halo_out[0], halo(0, q))
            when_start(halo_out[1], halo(1, q))

    if not last:
        for q in range(HALVES):
            update(q)
    for h in halves:
        if pieces == n_row:
            finish_piece(h)
        else:
            pl.when(owns)(functools.partial(finish_piece, h))
    for h in halves:
        for d in range(1, n_row):
            copy = gather(h, "row", d)
            if pieces == n_row:
                copy.wait_recv()
            else:
                when_recv((row + n_row - d) % n_row < pieces, copy)
        for d in range(1, n_col):
            gather(h, "col", d).start()
        update(h if last else HALVES + h)
    for h in halves:
        for d in range(1, n_col):
            gather(h, "col", d).wait_recv()
        for d in range(1, n_sub):
            gather(h, "sub", d).start()
    for q in range(HALVES if last else 2 * HALVES, CHUNKS):
        update(q)
    if not last:
        for q in range(CHUNKS):
            when_recv(halo_in[0], halo(0, q))
            when_start(halo_out[2], halo(2, q))
    for h in halves:
        for d in range(1, n_sub):
            gather(h, "sub", d).wait_recv()
    if not last:
        for q in range(CHUNKS):
            when_recv(halo_in[1], halo(1, q))
            when_recv(halo_in[2], halo(2, q))

    for q in range(CHUNKS):
        for kind in range(3):
            pl.when(spill_out[kind])(lambda copy=spill(kind, q): copy.wait_send())
            if not last:
                pl.when(halo_out[kind])(lambda copy=halo(kind, q): copy.wait_send())
    for h in halves:
        for d in range(1, n_sub):
            scatter_sub(h, d).wait_send()
            gather(h, "sub", d).wait_send()
        for d in range(1, n_col):
            scatter_col(h, d).wait_send()
            gather(h, "col", d).wait_send()
        for d in range(1, n_row):
            for cond, copy in (((row + d) % n_row < pieces, scatter_row(h, d)), (owns, gather(h, "row", d))):
                if pieces == n_row:
                    copy.wait_send()
                else:
                    pl.when(cond)(lambda copy=copy: copy.wait_send())


def solution(mesh):
    n_row, n_col, n_sub = mesh.shape["row"], mesh.shape["col"], mesh.shape["sub"]

    def local(
        object_field, probe_field, patterns, offset_rows, offset_cols, counts, fresnel, object_step, probe_step
    ):
        n = probe_field.shape[1]
        sub_rows = n // HALVES // n_sub
        col_rows = sub_rows // n_col
        row_rows = col_rows // min(n_row, col_rows // 8)
        f32 = jnp.float32
        dma = pltpu.SemaphoreType.DMA
        smem = pl.BlockSpec(memory_space=pltpu.SMEM)
        vmem = pl.BlockSpec(memory_space=pltpu.VMEM)
        sizes = (n_row, n_col, n_sub)
        region_shape = jax.ShapeDtypeStruct((2, 2 * n, 2 * n), f32)
        tile_shape = jax.ShapeDtypeStruct((2, n, n), f32)
        tile_scratch = pltpu.VMEM((2, n, n), f32)
        limit = 28 * 1024 * 1024
        cost = pl.CostEstimate(flops=6_000_000_000, bytes_accessed=8_000_000, transcendentals=0)
        copies = [dma((3, CHUNKS)), dma((3, CHUNKS))]

        region, left, right = pl.pallas_call(
            functools.partial(exchange_first, sizes),
            out_shape=(
                region_shape,
                jax.ShapeDtypeStruct((2 * n, 6 * n), jnp.bfloat16),
                jax.ShapeDtypeStruct((3 * n, 2 * n), jnp.bfloat16),
            ),
            in_specs=[smem, vmem],
            out_specs=(vmem, vmem, vmem),
            scratch_shapes=copies,
            cost_estimate=cost,
            compiler_params=pltpu.CompilerParams(
                collective_id=0, has_side_effects=True, vmem_limit_bytes=limit
            ),
        )(fresnel, object_field)

        probe = probe_field
        for it in range(ITERS):
            last = it == ITERS - 1
            grad, partial = pl.pallas_call(
                functools.partial(gradients, sizes),
                out_shape=(region_shape, jax.ShapeDtypeStruct((3, n, n), f32)),
                in_specs=[smem] * 3 + [vmem] * 5,
                out_specs=(vmem, vmem),
                scratch_shapes=[
                    pltpu.VMEM((2 * patterns.shape[0], 3 * n, 2 * n), f32),
                    pltpu.VMEM((2 * patterns.shape[0], 6 * n, n), jnp.bfloat16),
                    pltpu.VMEM((2 * patterns.shape[0], n, n), f32),
                ],
                cost_estimate=cost,
                compiler_params=pltpu.CompilerParams(vmem_limit_bytes=limit),
            )(offset_rows, offset_cols, counts, region, probe, patterns, left, right)
            region, probe = pl.pallas_call(
                functools.partial(exchange_next, sizes, last),
                out_shape=(tile_shape if last else region_shape, tile_shape),
                in_specs=[smem] * 2 + [vmem] * 4,
                out_specs=(vmem, vmem),
                scratch_shapes=[
                    tile_scratch,
                    tile_scratch,
                    pltpu.VMEM((HALVES, 3, sub_rows, n), f32),
                    tile_scratch,
                    tile_scratch,
                    tile_scratch,
                    pltpu.VMEM((HALVES, n_sub - 1, 3, sub_rows, n), f32),
                    pltpu.VMEM((HALVES, n_col - 1, 3, col_rows, n), f32),
                    pltpu.VMEM((HALVES, n_row - 1, 3, row_rows, n), f32),
                ]
                + copies
                + copies
                + [dma((HALVES, 2, count - 1)) for count in (n_sub, n_sub, n_col, n_col, n_row, n_row)],
                cost_estimate=cost,
                compiler_params=pltpu.CompilerParams(
                    collective_id=1 + it, has_side_effects=True, vmem_limit_bytes=limit
                ),
            )(object_step, probe_step, region, probe, grad, partial)
        return region, probe

    owners = ("groups", "row", "col", "sub")
    tiled = P(None, ("groups", "row", "sub"), "col")
    probes = P("groups", None, None)
    return jax.shard_map(
        local,
        mesh=mesh,
        in_specs=(tiled, probes, P(owners, None, None), P(owners), P(owners), P(owners), P(), P(), P()),
        out_specs=(tiled, probes),
        check_vma=False,
    )
```
